32 devices in a mesh: kv: 4 (over y, x), sp: 8 (over z, core).
Axes of the slice: x: 2, y: 2, z: 4, core: 2. Of those that a mesh axis runs over, the one named last changes fastest.
Arguments:
- queries: bfloat16 [4096, 4096], P('sp'), may hold values from -1.1953125 to 1.1953125
- keys: bfloat16 [8192, 4096], P(('kv', 'sp')), may hold values from -1.1953125 to 1.1953125
- values: bfloat16 [8192, 4096], P(('kv', 'sp')), may hold values from -6 to 6
- outputs: bfloat16 [4096, 4096], P('sp'), may hold values from -6 to 6
- out_grad: bfloat16 [4096, 4096], P('sp'), may hold values from -768 to 768
- stats: float32 [4096, 32], P('sp'), may hold values from -1 to 1
Outputs:
- query_grad: float32 [4096, 4096], P(('kv', 'sp'))
- key_grad: float32 [8192, 4096], P(('kv', 'sp'))
- value_grad: float32 [8192, 4096], P(('kv', 'sp'))
The draws below stay inside these ranges and needn't reach their ends.
All inputs are finite; a program needn't handle non-finite values.
Results may differ from the reference program's by a relative error of at most 0.0029.
Values may be sent and summed in bfloat16 or wider, within the bound.
A program may use at most 128 MiB of HBM per device.

```python
import math
import jax
import jax.numpy as jnp
from jax import lax

H = 32
DH = 128
QLEN = 4096
KEYS = 8192
N_KV = 4


def levels(rng, dims, cuts, smallest, largest):
    level, own = 1.0, jax.random.fold_in(rng, 6)
    for position, parts in cuts:
        draws = jnp.exp(jax.random.uniform(jax.random.fold_in(own, position), (parts,), jnp.float32, smallest / len(cuts), largest / len(cuts)))
        level = level * jnp.repeat(draws, dims[position] // parts).reshape([-1 if axis == position else 1 for axis in range(len(dims))])
    return level


def bell_draw(stream_key, shape, width, most, shards=(), held_as=jnp.bfloat16):
    factor_of = levels(stream_key, shape, shards, -0.22, 0.18) if shards else 1.0
    values = jax.random.normal(stream_key, shape, jnp.float32) * width * factor_of
    return jnp.minimum(jnp.maximum(values, -most), most).astype(held_as)


def setup_inputs(seed: int = 0) -> dict:
    key_list = jax.random.split(jax.random.key(seed), 7)
    queries = jnp.clip(jax.random.uniform(key_list[0], (QLEN, H * DH), jnp.float32, -1.1953125, 1.1953125) * levels(key_list[0], (QLEN, H * DH), ((0, 8),), -0.4, 0.0), -1.1953125, 1.1953125).astype(jnp.bfloat16)
    keys = jnp.clip(jax.random.uniform(key_list[1], (KEYS, H * DH), jnp.float32, -1.1953125, 1.1953125) * levels(key_list[1], (KEYS, H * DH), ((0, 32),), -0.4, 0.0), -1.1953125, 1.1953125).astype(jnp.bfloat16)
    values = bell_draw(key_list[2], (KEYS, H * DH), 1.0, 6.0, ((0, 32),))
    outputs = bell_draw(key_list[3], (QLEN, H * DH), 1.0, 6.0, ((0, 8),))
    out_grad = bell_draw(key_list[4], (QLEN, H * DH), (32 * N_KV), 768.0, ((0, 8),))
    stats = jnp.clip(jax.random.uniform(key_list[5], (QLEN, H), jnp.float32, -1.0, 1.0) * levels(key_list[5], (QLEN, H), ((0, 8),), -0.4, 0.0), -1.0, 1.0)
    return {"queries": queries, "keys": keys, "values": values, "outputs": outputs, "out_grad": out_grad, "stats": stats}


def head_major(array):
    return jnp.transpose(array.reshape(array.shape[0], H, DH), (1, 0, 2))

def reference(queries, keys, values, outputs, out_grad, stats):
    inverse_root = 1.0 / math.sqrt(DH)
    delta = lax.optimization_barrier(jnp.sum(out_grad.astype(jnp.float32).reshape(QLEN, H, DH) * outputs.astype(jnp.float32).reshape(QLEN, H, DH), axis=2))

    def one_head(pieces):
        query_head, key_head, value_head, grad_head, stats_head, delta_head = pieces
        query_wide = query_head.astype(jnp.float32)
        key_wide = key_head.astype(jnp.float32)
        value_wide = value_head.astype(jnp.float32)
        grad_wide = grad_head.astype(jnp.float32)
        scores = jnp.dot(query_wide, key_wide.T, preferred_element_type=jnp.float32) * inverse_root
        probs = jnp.exp(scores - stats_head[:, None]) / KEYS
        probs_low = probs.astype(jnp.bfloat16).astype(jnp.float32)
        value_out = jnp.dot(probs_low.T, grad_wide, preferred_element_type=jnp.float32)
        prob_grad = jnp.dot(grad_wide, value_wide.T, preferred_element_type=jnp.float32)
        score_grad = (probs * (prob_grad - delta_head[:, None])).astype(jnp.bfloat16).astype(jnp.float32)
        query_out = jnp.dot(score_grad, key_wide, preferred_element_type=jnp.float32) * inverse_root
        key_out = jnp.dot(score_grad.T, query_wide, preferred_element_type=jnp.float32) * inverse_root
        return (query_out, key_out, value_out)
    query_all, key_all, value_all = lax.map(one_head, (head_major(queries), head_major(keys), head_major(values), head_major(out_grad), jnp.transpose(stats), jnp.transpose(delta)))
    query_grad = jnp.transpose(query_all, (1, 0, 2)).reshape(QLEN, H * DH)
    key_grad = jnp.transpose(key_all, (1, 0, 2)).reshape(KEYS, H * DH)
    value_grad = jnp.transpose(value_all, (1, 0, 2)).reshape(KEYS, H * DH)
    return (query_grad, key_grad, value_grad)
```

```python
import functools
import math

import jax
import jax.numpy as jnp
from jax import lax
from jax.experimental import pallas as pl
from jax.experimental.pallas import tpu as pltpu
from jax.sharding import Mesh, PartitionSpec as P

DH = 128
NT = (((1,), (1,)), ((), ()))
NN = (((1,), (0,)), ((), ()))
TN = (((0,), (0,)), ((), ()))


def dot(left, right, dims):
    return lax.dot_general(left, right, dims, preferred_element_type=jnp.float32)


def attention_kernel(qt, kt, key_total, st_ref, de_ref, q_ref, g_ref, k_ref, v_ref, dq_ref, dk_ref, dv_ref, dk_acc, dv_acc):
    inverse_root = 1.0 / math.sqrt(DH)
    to_log2 = math.log2(math.e)
    dk_acc[...] = jnp.zeros_like(dk_acc)
    dv_acc[...] = jnp.zeros_like(dv_acc)

    def q_step(i, carry):
        qs = pl.ds(pl.multiple_of(i * qt, qt), qt)
        q = q_ref[qs, :]
        g = g_ref[qs, :]
        st = st_ref[0, :, qs] * to_log2 + math.log2(key_total)
        de = de_ref[0, :, qs]
        total = None
        for j in range(k_ref.shape[0] // kt):
            ks = pl.ds(j * kt, kt)
            k = k_ref[ks, :]
            probs = jnp.exp2(dot(k, q, NT) * (inverse_root * to_log2) - st)
            dv_acc[ks, :] += dot(probs.astype(jnp.bfloat16), g, NN)
            prob_grad = dot(v_ref[ks, :], g, NT)
            ds = (probs * (prob_grad - de)).astype(jnp.bfloat16)
            dk_acc[ks, :] += dot(ds, q, NN)
            part = dot(k, ds, TN)
            total = part if total is None else total + part
        dq_ref[qs, :] = (total * inverse_root).T.astype(dq_ref.dtype)
        return carry

    lax.fori_loop(0, q_ref.shape[0] // qt, q_step, 0)
    dk_ref[...] = (dk_acc[...] * inverse_root).astype(dk_ref.dtype)
    dv_ref[...] = dv_acc[...].astype(dv_ref.dtype)


def attention(q, g, k, v, st, de, key_total, dq_type):
    rows, width = q.shape
    keys = k.shape[0]
    heads = width // DH

    def columns(n):
        return pl.BlockSpec((n, DH), lambda h: (0, h))

    row = pl.BlockSpec((1, 1, rows), lambda h: (h, 0, 0))
    return pl.pallas_call(
        functools.partial(attention_kernel, min(1024, rows), min(256, keys), key_total),
        grid=(heads,),
        in_specs=[row, row, columns(rows), columns(rows), columns(keys), columns(keys)],
        out_specs=[columns(rows), columns(keys), columns(keys)],
        out_shape=[
            jax.ShapeDtypeStruct((rows, width), dq_type),
            jax.ShapeDtypeStruct((keys, width), jnp.bfloat16),
            jax.ShapeDtypeStruct((keys, width), jnp.bfloat16),
        ],
        scratch_shapes=[pltpu.VMEM((keys, DH), jnp.float32)] * 2,
        compiler_params=pltpu.CompilerParams(vmem_limit_bytes=40 * 2**20),
    )(st, de, q, g, k, v)


def row_products(left, right, heads):
    rows = left.shape[0]
    return jnp.sum(
        left.astype(jnp.float32).reshape(rows, heads, -1)
        * right.astype(jnp.float32).reshape(rows, heads, -1),
        axis=2,
    )


def on_device(queries, keys, values, outputs, out_grad, stats):
    kv_n, z_n, c_n = lax.axis_size("kv"), lax.axis_size("z"), lax.axis_size("c")
    heads = stats.shape[1]
    key_total = keys.shape[0] * kv_n * z_n * c_n
    q_len = queries.shape[0] * z_n * c_n
    delta = row_products(out_grad, outputs, heads)
    kv = lax.axis_index("kv")

    def to_heads(array):
        width = array.shape[1] // kv_n
        own = lax.dynamic_slice_in_dim(array, kv * width, width, 1)
        pair = lax.all_to_all(own, "c", split_axis=1, concat_axis=0, tiled=True)
        return lax.all_gather(pair, "z", axis=0, tiled=True)

    def exchange(array):
        return lax.all_to_all(array, ("kv", "c"), split_axis=1, concat_axis=0, tiled=True)

    def give_back(array):
        return lax.all_to_all(array, ("kv", "c"), split_axis=0, concat_axis=1, tiled=True)

    k, v = exchange(keys), exchange(values)
    q, g = to_heads(queries), to_heads(out_grad)
    both = jnp.stack([stats, delta], axis=1).reshape(-1, 2, heads)
    width = heads // kv_n
    both = lax.dynamic_slice_in_dim(both, kv * width, width, 2)
    both = lax.all_gather(both, ("z", "c"), axis=0, tiled=True)
    width //= c_n
    both = lax.dynamic_slice_in_dim(both, lax.axis_index("c") * width, width, 2)
    st = jnp.transpose(both[:, 0])[:, None, :]
    de = jnp.transpose(both[:, 1])[:, None, :]
    dq, dk, dv = attention(q, g, k, v, st, de, key_total, jnp.float32)
    part = dq.reshape(kv_n, z_n, c_n, q_len // (kv_n * z_n * c_n), dq.shape[1])
    part = lax.psum_scatter(part, "z", scatter_dimension=1, tiled=True)
    dq = give_back(part.reshape(-1, dq.shape[1]).astype(jnp.bfloat16))
    dk, dv = give_back(dk), give_back(dv)
    return tuple(array.astype(jnp.float32) for array in (dq, dk, dv))


def solution(mesh):
    kv_n, sp_n = mesh.shape["kv"], mesh.shape["sp"]
    mesh = Mesh(mesh.devices.reshape(kv_n, sp_n // 2, 2), ("kv", "z", "c"))
    sp = P(("z", "c"), None)
    both = P(("kv", "z", "c"), None)
    return jax.shard_map(
        on_device,
        mesh=mesh,
        in_specs=(sp, both, both, sp, sp, sp),
        out_specs=(both, both, both),
        check_vma=False,
    )
```

```python
import functools
import math

import jax
import jax.numpy as jnp
from jax import lax
from jax.experimental import pallas as pl
from jax.experimental.pallas import tpu as pltpu
from jax.sharding import Mesh, PartitionSpec as P

DH = 128
NT = (((1,), (1,)), ((), ()))
NN = (((1,), (0,)), ((), ()))
TN = (((0,), (0,)), ((), ()))


def dot(left, right, dims):
    return lax.dot_general(left, right, dims, preferred_element_type=jnp.float32)


MESH = pl.DeviceIdType.MESH


def fused_kernel(key_total, q_in, g_in, k_in, v_in, aux_in, dq_out, dk_out, dv_out,
                 q_buf, g_buf, aux_buf, k_buf, v_buf, dq_stage, dk_stage, dv_stage, dk_acc, dv_acc,
                 kv_recv, kv_send, row_recv, own_send, mate_send, pass_send,
                 aux_recv, aux_own, aux_mate, aux_pass, out_recv, out_send):
    kv_n, z_n, c_n = lax.axis_size("kv"), lax.axis_size("z"), lax.axis_size("c")
    kv, z, c = lax.axis_index("kv"), lax.axis_index("z"), lax.axis_index("c")
    groups = kv_n * c_n
    count = groups * z_n
    group = kv * c_n + c
    heads = q_buf.shape[0]
    part = q_in.shape[0]
    owned = dq_out.shape[1]
    inverse_root = 1.0 / math.sqrt(DH)
    to_log2 = math.log2(math.e)
    width = heads * DH
    rows_io = ((q_in, q_buf), (g_in, g_buf))
    keys_io = ((k_in, k_buf), (v_in, v_buf))
    grads_io = ((dk_stage, dk_out), (dv_stage, dv_out))

    def device(index):
        inner = lax.rem(index, z_n * c_n)
        return (index // (z_n * c_n), inner // c_n, lax.rem(inner, c_n))

    def send(src, dst, s, r, where):
        return pltpu.make_async_remote_copy(src, dst, s, r, device_id=where, device_id_type=MESH)

    def cols(owner, h):
        return pl.ds(pl.multiple_of(owner * width + h * DH, DH), DH)

    barrier = pltpu.get_barrier_semaphore()
    me = (kv * z_n + z) * c_n + c

    def greet(i, carry):
        pl.semaphore_signal(barrier, inc=1, device_id=device(lax.rem(me + i, count)), device_id_type=MESH)
        return carry

    lax.fori_loop(1, count, greet, 0)
    pl.semaphore_wait(barrier, count - 1)

    my_rows = pl.ds(pl.multiple_of(c * part, part), part)

    def send_keys(h):
        for a, (src, buf) in enumerate(keys_io):
            pltpu.make_async_copy(src.at[:, cols(group, h)], buf.at[h, group], kv_recv.at[h, a]).start()

        def one(i, carry):
            peer = lax.rem(group + i, groups)
            for a, (src, buf) in enumerate(keys_io):
                send(src.at[:, cols(peer, h)], buf.at[h, group], kv_send.at[a], kv_recv.at[h, a],
                     (peer // c_n, z, lax.rem(peer, c_n))).start()
            return carry

        lax.fori_loop(1, groups, one, 0)

    def send_rows(h):
        for a, (src, buf) in enumerate(rows_io):
            land = buf.at[h, z, my_rows]
            pltpu.make_async_copy(src.at[:, cols(group, h)], land, row_recv.at[h, z, a]).start()
            mate = 1 - c
            send(src.at[:, cols(kv * c_n + mate, h)], land, mate_send.at[a], row_recv.at[h, z, a],
                 (kv, z, mate)).start()
        for side, ok, there in sides:
            @pl.when(ok)
            def _():
                for a, (src, buf) in enumerate(rows_io):
                    for cc in range(c_n):
                        send(src.at[:, cols(kv * c_n + cc, h)], buf.at[h, z, my_rows], own_send.at[side, a],
                             row_recv.at[h, z, a], (kv, there, cc)).start()

    sides = ((0, z > 0, z - 1), (1, z < z_n - 1, z + 1))

    pltpu.make_async_copy(aux_in.at[c], aux_buf.at[z, c], aux_recv.at[z]).start()
    send(aux_in.at[1 - c], aux_buf.at[z, c], aux_mate, aux_recv.at[z], (kv, z, 1 - c)).start()
    for side, ok, there in sides:
        @pl.when(ok)
        def _():
            for cc in range(c_n):
                send(aux_in.at[cc], aux_buf.at[z, c], aux_own.at[side], aux_recv.at[z], (kv, there, cc)).start()

    send_keys(0)
    send_rows(0)
    if heads > 1:
        send_keys(1)
        send_rows(1)

    def unit(h, zz):
        q = q_buf[h, zz]
        g = g_buf[h, zz]
        st = jnp.concatenate([aux_buf[zz, i, pl.ds(2 * h, 1), :] for i in range(c_n)], axis=1)
        de = jnp.concatenate([aux_buf[zz, i, pl.ds(2 * h + 1, 1), :] for i in range(c_n)], axis=1)
        st = st * to_log2 + math.log2(key_total)

        def k_step(j, total):
            k = k_buf[h, j]
            probs = jnp.exp2(dot(k, q, NT) * (inverse_root * to_log2) - st)
            dv_acc[j] += dot(probs.astype(jnp.bfloat16), g, NN)
            prob_grad = dot(v_buf[h, j], g, NT)
            ds = (probs * (prob_grad - de)).astype(jnp.bfloat16)
            dk_acc[j] += dot(ds, q, NN)
            return total + dot(k, ds, TN)

        total = lax.fori_loop(0, groups, k_step, jnp.zeros((DH, q.shape[0]), jnp.float32), unroll=True)
        out = (total * inverse_root).T.astype(dq_stage.dtype)
        dq_stage[h, pl.ds(zz * groups, groups)] = out.reshape(groups, owned, DH)

        def push(j, carry):
            piece = zz * groups + j
            src, dst = dq_stage.at[h, piece], dq_out.at[z, :, cols(group, h)]

            @pl.when(piece == me)
            def _():
                pltpu.make_async_copy(src, dst, out_recv.at[2]).start()

            @pl.when(piece != me)
            def _():
                send(src, dst, out_send.at[2], out_recv.at[2], device(piece)).start()

            return carry

        lax.fori_loop(0, groups, push, 0)

    def at_offset(t):
        near = (t + 1) // 2
        left = lax.rem(t, 2) == 1
        zz = jnp.where(left, z - near, z + near)
        there = jnp.where(left, z + 1, z - 1)
        valid = (zz >= 0) & (zz < z_n)
        onward = valid & (t > 0) & (there >= 0) & (there < z_n)
        return zz, there, valid, onward

    def passes(h, zz, there):
        return [send(buf.at[h, zz], buf.at[h, zz], pass_send.at[h, zz, a], row_recv.at[h, zz, a], (kv, there, c))
                for a, (_, buf) in enumerate(rows_io)]

    def aux_passes(zz, there):
        return send(aux_buf.at[zz], aux_buf.at[zz], aux_pass.at[zz], aux_recv.at[zz], (kv, there, c))

    def arrived(ref, sem):
        pltpu.make_async_copy(ref, ref, sem).wait()

    def head(h, carry):
        @pl.when(h + 2 < heads)
        def _():
            send_keys(h + 2)
            send_rows(h + 2)

        dk_acc[...] = jnp.zeros_like(dk_acc)
        dv_acc[...] = jnp.zeros_like(dv_acc)
        for a, (_, buf) in enumerate(keys_io):
            arrived(buf.at[h], kv_recv.at[h, a])

        def step(t, inner):
            zz, there, valid, onward = at_offset(t)

            @pl.when(valid)
            def _():
                for a, (_, buf) in enumerate(rows_io):
                    arrived(buf.at[h, zz], row_recv.at[h, zz, a])

                @pl.when(h == 0)
                def _():
                    arrived(aux_buf.at[zz], aux_recv.at[zz])

                @pl.when(onward)
                def _():
                    for copy in passes(h, zz, there):
                        copy.start()

                    @pl.when(h == 0)
                    def _():
                        aux_passes(zz, there).start()

                unit(h, zz)

            return inner

        lax.fori_loop(0, 2 * z_n - 1, step, 0)
        dk_stage[h] = (dk_acc[...] * inverse_root).astype(dk_stage.dtype)
        dv_stage[h] = dv_acc[...].astype(dv_stage.dtype)
        for a, (stage, out) in enumerate(grads_io):
            pltpu.make_async_copy(stage.at[h, group], out.at[:, cols(group, h)], out_recv.at[a]).start()

        def one(i, inner):
            peer = lax.rem(group + i, groups)
            for a, (stage, out) in enumerate(grads_io):
                send(stage.at[h, peer], out.at[:, cols(group, h)], out_send.at[a], out_recv.at[a],
                     (peer // c_n, z, lax.rem(peer, c_n))).start()
            return inner

        lax.fori_loop(1, groups, one, 0)
        return carry

    lax.fori_loop(0, heads, head, 0)

    for a, (src, buf) in enumerate(rows_io):
        arrived(src.at[:, pl.ds(0, width)], mate_send.at[a])
        for side, ok, there in sides:
            @pl.when(ok)
            def _():
                arrived(src.at[:, pl.ds(0, c_n * width)], own_send.at[side, a])
    arrived(aux_in.at[0], aux_mate)
    for side, ok, there in sides:
        @pl.when(ok)
        def _():
            arrived(aux_in, aux_own.at[side])
    for a, (_, buf) in enumerate(keys_io):
        arrived(buf.at[:, pl.ds(0, groups - 1)], kv_send.at[a])

    def finish(h, carry):
        def step(t, inner):
            zz, there, valid, onward = at_offset(t)

            @pl.when(onward)
            def _():
                for copy in passes(h, zz, there):
                    copy.wait_send()

                @pl.when(h == 0)
                def _():
                    aux_passes(zz, there).wait_send()

            return inner

        return lax.fori_loop(0, 2 * z_n - 1, step, carry)

    lax.fori_loop(0, heads, finish, 0)
    for a, (stage, out) in enumerate(grads_io):
        arrived(stage.at[:, pl.ds(0, groups - 1)], out_send.at[a])
        arrived(out, out_recv.at[a])
    arrived(dq_stage.at[:, pl.ds(0, count - 1)], out_send.at[2])
    arrived(dq_out, out_recv.at[2])


def fused(q, g, k, v, aux, key_total, kv_n, z_n, c_n):
    part, total = q.shape
    groups = kv_n * c_n
    heads = total // DH // groups
    keys = k.shape[0]
    owned = part // kv_n
    low = jnp.bfloat16
    dma = pltpu.SemaphoreType.DMA
    any_space = pl.BlockSpec(memory_space=pl.ANY)
    return pl.pallas_call(
        functools.partial(fused_kernel, key_total),
        in_specs=[any_space] * 5,
        out_specs=[any_space] * 3,
        out_shape=[
            jax.ShapeDtypeStruct((z_n, owned, total), low),
            jax.ShapeDtypeStruct((keys, total), low),
            jax.ShapeDtypeStruct((keys, total), low),
        ],
        scratch_shapes=[pltpu.VMEM((heads, z_n, c_n * part, DH), low)] * 2
        + [pltpu.VMEM((z_n, c_n) + aux.shape[1:], jnp.float32)]
        + [pltpu.VMEM((heads, groups, keys, DH), low)] * 2
        + [pltpu.VMEM((heads, z_n * groups, owned, DH), low)]
        + [pltpu.VMEM((heads, groups, keys, DH), low)] * 2
        + [pltpu.VMEM((groups, keys, DH), jnp.float32)] * 2
        + [
            dma((heads, 2)), dma((2,)), dma((heads, z_n, 2)), dma((2, 2)), dma((2,)), dma((heads, z_n, 2)),
            dma((z_n,)), dma((2,)), dma, dma((z_n,)), dma((3,)), dma((3,)),
        ],
        compiler_params=pltpu.CompilerParams(
            collective_id=0, has_side_effects=True, vmem_limit_bytes=48 * 2**20
        ),
        cost_estimate=pl.CostEstimate(flops=43 * 10**9, bytes_accessed=3 * 10**7, transcendentals=0),
    )(q, g, k, v, aux)


def row_products(left, right, heads):
    rows = left.shape[0]
    return jnp.sum(
        left.astype(jnp.float32).reshape(rows, heads, -1)
        * right.astype(jnp.float32).reshape(rows, heads, -1),
        axis=2,
    )


def on_device(queries, keys, values, outputs, out_grad, stats):
    kv_n, z_n, c_n = lax.axis_size("kv"), lax.axis_size("z"), lax.axis_size("c")
    heads = stats.shape[1]
    key_total = keys.shape[0] * kv_n * z_n * c_n
    kv = lax.axis_index("kv")
    width = queries.shape[1] // kv_n
    near = heads // kv_n

    def own(array, size):
        return lax.dynamic_slice_in_dim(array, kv * size, size, 1)

    delta = row_products(own(out_grad, width), own(outputs, width), near)
    aux = jnp.stack([own(stats, near).T, delta.T], axis=1)
    aux = aux.reshape(c_n, 2 * near // c_n, stats.shape[0])
    dq, dk, dv = fused(queries, out_grad, keys, values, aux, key_total, kv_n, z_n, c_n)
    return jnp.sum(dq.astype(jnp.float32), axis=0), dk.astype(jnp.float32), dv.astype(jnp.float32)


def solution(mesh):
    kv_n, sp_n = mesh.shape["kv"], mesh.shape["sp"]
    mesh = Mesh(mesh.devices.reshape(kv_n, sp_n // 2, 2), ("kv", "z", "c"))
    sp = P(("z", "c"), None)
    both = P(("kv", "z", "c"), None)
    return jax.shard_map(
        on_device,
        mesh=mesh,
        in_specs=(sp, both, both, sp, sp, sp),
        out_specs=(both, both, both),
        check_vma=False,
    )
```

```python
import functools
import math

import jax
import jax.numpy as jnp
from jax import lax
from jax.experimental import pallas as pl
from jax.experimental.pallas import tpu as pltpu
from jax.sharding import Mesh, PartitionSpec as P

DH = 128
NT = (((1,), (1,)), ((), ()))
NN = (((1,), (0,)), ((), ()))
TN = (((0,), (0,)), ((), ()))


def dot(left, right, dims):
    return lax.dot_general(left, right, dims, preferred_element_type=jnp.float32)


MESH = pl.DeviceIdType.MESH


def fused_kernel(key_total, q_in, g_in, k_in, v_in, aux_in, dq_out, dk_out, dv_out,
                 q_buf, g_buf, aux_buf, k_buf, v_buf, dq_stage, dq_send, dq_recv, dk_stage, dv_stage, dk_acc, dv_acc,
                 kv_recv, kv_send, row_recv, own_send, mate_send, pass_send,
                 aux_recv, aux_own, aux_mate, aux_pass, out_recv, out_send, sum_recv, sum_send,
                 dq_out_recv, dq_out_send):
    kv_n, z_n, c_n = lax.axis_size("kv"), lax.axis_size("z"), lax.axis_size("c")
    kv, z, c = lax.axis_index("kv"), lax.axis_index("z"), lax.axis_index("c")
    groups = kv_n * c_n
    count = groups * z_n
    group = kv * c_n + c
    heads = q_buf.shape[0]
    part = q_in.shape[0]
    owned = dq_out.shape[1]
    inverse_root = 1.0 / math.sqrt(DH)
    to_log2 = math.log2(math.e)
    width = heads * DH
    rows_io = ((q_in, q_buf), (g_in, g_buf))
    keys_io = ((k_in, k_buf), (v_in, v_buf))
    grads_io = ((dk_stage, dk_out), (dv_stage, dv_out))

    def device(index):
        inner = lax.rem(index, z_n * c_n)
        return (index // (z_n * c_n), inner // c_n, lax.rem(inner, c_n))

    def send(src, dst, s, r, where):
        return pltpu.make_async_remote_copy(src, dst, s, r, device_id=where, device_id_type=MESH)

    def cols(owner, h):
        return pl.ds(pl.multiple_of(owner * width + h * DH, DH), DH)

    barrier = pltpu.get_barrier_semaphore()
    me = (kv * z_n + z) * c_n + c

    def greet(i, carry):
        pl.semaphore_signal(barrier, inc=1, device_id=device(lax.rem(me + i, count)), device_id_type=MESH)
        return carry

    lax.fori_loop(1, count, greet, 0)
    pl.semaphore_wait(barrier, count - 1)

    my_rows = pl.ds(pl.multiple_of(c * part, part), part)

    def send_keys(h):
        for a, (src, buf) in enumerate(keys_io):
            pltpu.make_async_copy(src.at[:, cols(group, h)], buf.at[h, group], kv_recv.at[h, a]).start()

        def one(i, carry):
            peer = lax.rem(group + i, groups)
            for a, (src, buf) in enumerate(keys_io):
                send(src.at[:, cols(peer, h)], buf.at[h, group], kv_send.at[a], kv_recv.at[h, a],
                     (peer // c_n, z, lax.rem(peer, c_n))).start()
            return carry

        lax.fori_loop(1, groups, one, 0)

    def send_rows(h):
        for a, (src, buf) in enumerate(rows_io):
            land = buf.at[h, z, my_rows]
            pltpu.make_async_copy(src.at[:, cols(group, h)], land, row_recv.at[h, z, a]).start()
            mate = 1 - c
            send(src.at[:, cols(kv * c_n + mate, h)], land, mate_send.at[a], row_recv.at[h, z, a],
                 (kv, z, mate)).start()
        for side, ok, there in sides:
            @pl.when(ok)
            def _():
                for a, (src, buf) in enumerate(rows_io):
                    for cc in range(c_n):
                        send(src.at[:, cols(kv * c_n + cc, h)], buf.at[h, z, my_rows], own_send.at[side, a],
                             row_recv.at[h, z, a], (kv, there, cc)).start()

    sides = ((0, z > 0, z - 1), (1, z < z_n - 1, z + 1))

    pltpu.make_async_copy(aux_in.at[c], aux_buf.at[z, c], aux_recv.at[z]).start()
    send(aux_in.at[1 - c], aux_buf.at[z, c], aux_mate, aux_recv.at[z], (kv, z, 1 - c)).start()
    for side, ok, there in sides:
        @pl.when(ok)
        def _():
            for cc in range(c_n):
                send(aux_in.at[cc], aux_buf.at[z, c], aux_own.at[side], aux_recv.at[z], (kv, there, cc)).start()

    send_keys(0)
    send_rows(0)
    if heads > 1:
        send_keys(1)
        send_rows(1)

    def unit(h, zz):
        q = q_buf[h, zz]
        g = g_buf[h, zz]
        st = jnp.concatenate([aux_buf[zz, i, pl.ds(2 * h, 1), :] for i in range(c_n)], axis=1)
        de = jnp.concatenate([aux_buf[zz, i, pl.ds(2 * h + 1, 1), :] for i in range(c_n)], axis=1)
        st = st * to_log2 + math.log2(key_total)

        def k_step(j, total):
            k = k_buf[h, j]
            probs = jnp.exp2(dot(k, q, NT) * (inverse_root * to_log2) - st)
            dv_acc[j] += dot(probs.astype(jnp.bfloat16), g, NN)
            prob_grad = dot(v_buf[h, j], g, NT)
            ds = (probs * (prob_grad - de)).astype(jnp.bfloat16)
            dk_acc[j] += dot(ds, q, NN)
            return total + dot(k, ds, TN)

        total = lax.fori_loop(0, groups, k_step, jnp.zeros((DH, q.shape[0]), jnp.float32), unroll=True)
        dq_stage[h, pl.ds(zz * groups, groups)] = (total * inverse_root).T.reshape(groups, owned, DH)

    def keep(h):
        def one(owner, carry):
            base = (owner * z_n + z) * c_n
            dq_send[h, pl.ds(base, c_n)] = dq_stage[h, pl.ds(base, c_n)].astype(dq_send.dtype)
            for cc in range(c_n):
                src, dst = dq_send.at[h, base + cc], dq_out.at[1, :, cols(group, h)]

                @pl.when(base + cc == me)
                def _():
                    pltpu.make_async_copy(src, dst, dq_out_recv.at[1]).start()

                @pl.when(base + cc != me)
                def _():
                    send(src, dst, dq_out_send.at[1], dq_out_recv.at[1], (owner, z, cc)).start()

            return carry

        lax.fori_loop(0, kv_n, one, 0)

    def toward(h, side):
        there = (z - 1, z + 1)[side]
        fed = (z < z_n - 1, z > 0)[side]
        slot = (2, 0)[side]

        def one(i, carry):
            owner, plane = i // z_n, lax.rem(i, z_n)

            @pl.when((plane < z, plane > z)[side])
            def _():
                base = (owner * z_n + plane) * c_n
                block = pl.ds(base, c_n)
                mine = dq_stage[h, block]

                @pl.when(fed)
                def _():
                    arrived(dq_recv.at[h, block], sum_recv.at[h, owner, plane])
                    dq_send[h, block] = (mine + dq_recv[h, block].astype(jnp.float32)).astype(dq_send.dtype)

                @pl.when(jnp.logical_not(fed))
                def _():
                    dq_send[h, block] = mine.astype(dq_send.dtype)

                @pl.when(plane == there)
                def _():
                    for cc in range(c_n):
                        send(dq_send.at[h, base + cc], dq_out.at[slot, :, cols(group, h)], dq_out_send.at[slot],
                             dq_out_recv.at[slot], (owner, there, cc)).start()

                @pl.when(plane != there)
                def _():
                    send(dq_send.at[h, block], dq_recv.at[h, block], sum_send.at[h, owner, plane],
                         sum_recv.at[h, owner, plane], (kv, there, c)).start()

            return carry

        lax.fori_loop(0, kv_n * z_n, one, 0)

    upper = 2 * z >= z_n

    def combine(h):
        @pl.when(upper)
        def _():
            toward(h, 0)

        toward(h, 1)

        @pl.when(jnp.logical_not(upper))
        def _():
            toward(h, 0)

    def at_offset(t):
        near = (t + 1) // 2
        left = lax.rem(t, 2) == 1
        zz = jnp.where(left, z - near, z + near)
        there = jnp.where(left, z + 1, z - 1)
        valid = (zz >= 0) & (zz < z_n)
        onward = valid & (t > 0) & (there >= 0) & (there < z_n)
        return zz, there, valid, onward

    def passes(h, zz, there):
        return [send(buf.at[h, zz], buf.at[h, zz], pass_send.at[h, zz, a], row_recv.at[h, zz, a], (kv, there, c))
                for a, (_, buf) in enumerate(rows_io)]

    def aux_passes(zz, there):
        return send(aux_buf.at[zz], aux_buf.at[zz], aux_pass.at[zz], aux_recv.at[zz], (kv, there, c))

    def arrived(ref, sem):
        pltpu.make_async_copy(ref, ref, sem).wait()

    def head(h, carry):
        @pl.when(h + 2 < heads)
        def _():
            send_keys(h + 2)
            send_rows(h + 2)

        dk_acc[...] = jnp.zeros_like(dk_acc)
        dv_acc[...] = jnp.zeros_like(dv_acc)
        for a, (_, buf) in enumerate(keys_io):
            arrived(buf.at[h], kv_recv.at[h, a])

        def step(t, inner):
            zz, there, valid, onward = at_offset(t)

            @pl.when(valid)
            def _():
                for a, (_, buf) in enumerate(rows_io):
                    arrived(buf.at[h, zz], row_recv.at[h, zz, a])

                @pl.when(h == 0)
                def _():
                    arrived(aux_buf.at[zz], aux_recv.at[zz])

                @pl.when(onward)
                def _():
                    for copy in passes(h, zz, there):
                        copy.start()

                    @pl.when(h == 0)
                    def _():
                        aux_passes(zz, there).start()

                unit(h, zz)

            return inner

        lax.fori_loop(0, 2 * z_n - 1, step, 0)
        dk_stage[h] = (dk_acc[...] * inverse_root).astype(dk_stage.dtype)
        dv_stage[h] = dv_acc[...].astype(dv_stage.dtype)
        for a, (stage, out) in enumerate(grads_io):
            pltpu.make_async_copy(stage.at[h, group], out.at[:, cols(group, h)], out_recv.at[a]).start()

        def one(i, inner):
            peer = lax.rem(group + i, groups)
            for a, (stage, out) in enumerate(grads_io):
                send(stage.at[h, peer], out.at[:, cols(group, h)], out_send.at[a], out_recv.at[a],
                     (peer // c_n, z, lax.rem(peer, c_n))).start()
            return inner

        lax.fori_loop(1, groups, one, 0)
        keep(h)
        late = h - lag

        @pl.when(late >= 0)
        def _():
            combine(late)

        return carry

    lag = jnp.where((z == 0) | (z == z_n - 1), 0, 1)
    lax.fori_loop(0, heads, head, 0)

    @pl.when(lag == 1)
    def _():
        combine(heads - 1)

    for a, (src, buf) in enumerate(rows_io):
        arrived(src.at[:, pl.ds(0, width)], mate_send.at[a])
        for side, ok, there in sides:
            @pl.when(ok)
            def _():
                arrived(src.at[:, pl.ds(0, c_n * width)], own_send.at[side, a])
    arrived(aux_in.at[0], aux_mate)
    for side, ok, there in sides:
        @pl.when(ok)
        def _():
            arrived(aux_in, aux_own.at[side])
    for a, (_, buf) in enumerate(keys_io):
        arrived(buf.at[:, pl.ds(0, groups - 1)], kv_send.at[a])

    def finish(h, carry):
        def step(t, inner):
            zz, there, valid, onward = at_offset(t)

            @pl.when(onward)
            def _():
                for copy in passes(h, zz, there):
                    copy.wait_send()

                @pl.when(h == 0)
                def _():
                    aux_passes(zz, there).wait_send()

            return inner

        return lax.fori_loop(0, 2 * z_n - 1, step, carry)

    lax.fori_loop(0, heads, finish, 0)
    for a, (stage, out) in enumerate(grads_io):
        arrived(stage.at[:, pl.ds(0, groups - 1)], out_send.at[a])
        arrived(out, out_recv.at[a])
    arrived(dq_send.at[:, pl.ds(0, groups - 1)], dq_out_send.at[1])
    arrived(dq_out.at[1], dq_out_recv.at[1])
    for side, ok, there in sides:
        @pl.when(ok)
        def _():
            slot = (2, 0)[side]
            arrived(dq_send.at[:, pl.ds(0, groups)], dq_out_send.at[slot])
            arrived(dq_out.at[(0, 2)[side]], dq_out_recv.at[(0, 2)[side]])

    def finish_sums(i, carry):
        h, rest = i // (kv_n * z_n), lax.rem(i, kv_n * z_n)
        owner, plane = rest // z_n, lax.rem(rest, z_n)

        @pl.when((plane < z - 1) | (plane > z + 1))
        def _():
            arrived(dq_send.at[h, pl.ds((owner * z_n + plane) * c_n, c_n)], sum_send.at[h, owner, plane])

        return carry

    lax.fori_loop(0, heads * kv_n * z_n, finish_sums, 0)


def fused(q, g, k, v, aux, key_total, kv_n, z_n, c_n):
    part, total = q.shape
    groups = kv_n * c_n
    heads = total // DH // groups
    keys = k.shape[0]
    owned = part // kv_n
    low = jnp.bfloat16
    dma = pltpu.SemaphoreType.DMA
    any_space = pl.BlockSpec(memory_space=pl.ANY)
    return pl.pallas_call(
        functools.partial(fused_kernel, key_total),
        in_specs=[any_space] * 5,
        out_specs=[any_space] * 3,
        out_shape=[
            jax.ShapeDtypeStruct((3, owned, total), low),
            jax.ShapeDtypeStruct((keys, total), low),
            jax.ShapeDtypeStruct((keys, total), low),
        ],
        scratch_shapes=[pltpu.VMEM((heads, z_n, c_n * part, DH), low)] * 2
        + [pltpu.VMEM((z_n, c_n) + aux.shape[1:], jnp.float32)]
        + [pltpu.VMEM((heads, groups, keys, DH), low)] * 2
        + [pltpu.VMEM((heads, z_n * groups, owned, DH), kind) for kind in (jnp.float32, low, low)]
        + [pltpu.VMEM((heads, groups, keys, DH), low)] * 2
        + [pltpu.VMEM((groups, keys, DH), jnp.float32)] * 2
        + [
            dma((heads, 2)), dma((2,)), dma((heads, z_n, 2)), dma((2, 2)), dma((2,)), dma((heads, z_n, 2)),
            dma((z_n,)), dma((2,)), dma, dma((z_n,)), dma((2,)), dma((2,)),
            dma((heads, kv_n, z_n)), dma((heads, kv_n, z_n)), dma((3,)), dma((3,)),
        ],
        compiler_params=pltpu.CompilerParams(
            collective_id=0, has_side_effects=True, vmem_limit_bytes=48 * 2**20
        ),
        cost_estimate=pl.CostEstimate(flops=43 * 10**9, bytes_accessed=3 * 10**7, transcendentals=0),
    )(q, g, k, v, aux)


def row_products(left, right, heads):
    rows = left.shape[0]
    return jnp.sum(
        left.astype(jnp.float32).reshape(rows, heads, -1)
        * right.astype(jnp.float32).reshape(rows, heads, -1),
        axis=2,
    )


def on_device(queries, keys, values, outputs, out_grad, stats):
    kv_n, z_n, c_n = lax.axis_size("kv"), lax.axis_size("z"), lax.axis_size("c")
    heads = stats.shape[1]
    key_total = keys.shape[0] * kv_n * z_n * c_n
    kv = lax.axis_index("kv")
    width = queries.shape[1] // kv_n
    near = heads // kv_n

    def own(array, size):
        return lax.dynamic_slice_in_dim(array, kv * size, size, 1)

    delta = row_products(own(out_grad, width), own(outputs, width), near)
    aux = jnp.stack([own(stats, near).T, delta.T], axis=1)
    aux = aux.reshape(c_n, 2 * near // c_n, stats.shape[0])
    dq, dk, dv = fused(queries, out_grad, keys, values, aux, key_total, kv_n, z_n, c_n)
    z = lax.axis_index("z")
    dq = dq.astype(jnp.float32)
    dq = dq[1] + jnp.where(z > 0, dq[0], 0.0) + jnp.where(z < z_n - 1, dq[2], 0.0)
    return dq, dk.astype(jnp.float32), dv.astype(jnp.float32)


def solution(mesh):
    kv_n, sp_n = mesh.shape["kv"], mesh.shape["sp"]
    mesh = Mesh(mesh.devices.reshape(kv_n, sp_n // 2, 2), ("kv", "z", "c"))
    sp = P(("z", "c"), None)
    both = P(("kv", "z", "c"), None)
    return jax.shard_map(
        on_device,
        mesh=mesh,
        in_specs=(sp, both, both, sp, sp, sp),
        out_specs=(both, both, both),
        check_vma=False,
    )
```
